32 devices in a mesh: groups: 2 (over y), row: 4 (over x, core), col: 4 (over z).
Axes of the slice: x: 2, y: 2, z: 4, core: 2. Of those that a mesh axis runs over, the one named last changes fastest.
Arguments:
- p_tiles: float32 [192, 512, 128], P(('groups', 'row'), 'col'), parts along dimension 0, may hold values from -0.5 to 0.5
- h_tiles: float32 [384, 512, 128], P(('groups', 'row'), 'col'), parts along dimension 0, may hold values from -6 to 6
- pair_lists: int32 [96, 384], P(('groups', 'row'), 'col'), parts along dimension 0, may hold values from 0 to 47, as said below
- pair_counts: int32 [32, 4], P(('groups', 'row'), 'col'), parts along dimension 0, may hold values from 48 to 96, as said below
Outputs:
- c_tiles: float32 [384, 512, 128], P(('groups', 'row'), 'col'), parts along dimension 0
The draws below stay inside these ranges and needn't reach their ends.
There are 2 independent parts, one for each index of `groups`. The reference program is written for one: setup_inputs(seed, part) draws one part's arguments, and reference() takes and returns one part's arrays. A program takes and returns all parts, laid end to end along the dimension named above; each array names one. Nothing has to cross between parts.
Inputs may be any that keep to these rules, and one draw needn't show every extreme that they name: `pair_lists`: entries of role 0 are slots of P below 24, of role 1 slots of H below 48, of role 2 slots of the product below 48; each role's largest slot is named somewhere. `pair_counts`: in every step some tile has 96 live products.
All inputs are finite; a program needn't handle non-finite values.
Results may differ from the reference program's by a relative error of at most 0.0003.
Values sent between devices are 32-bit elements; how exact they have to be, the bound alone decides.
A program may use at most 128 MiB of HBM per device.

```python
import jax
import jax.numpy as jnp
from jax import lax

BLK = 128
CAPA = 24
STEPS = 4
CAPB = 48
CAPC = 48
PAIRS = 96
N_ROW = 4
N_COL = 4


def draw_pair_lists(key, part):
    key = jax.random.fold_in(key, 11)
    grid_shape = (N_ROW * STEPS * 3, N_COL * PAIRS)
    random_bits = jax.random.randint(key, grid_shape, 0, 1 << 20)
    role_index = lax.broadcasted_iota(jnp.int32, grid_shape, 0) % 3
    column_index = lax.broadcasted_iota(jnp.int32, grid_shape, 1)
    upper = jnp.where(role_index == 0, CAPA, jnp.where(role_index == 1, CAPB, CAPC))
    slots = random_bits % upper
    slots = jnp.where(column_index == 0, upper - 1, slots)
    return slots.astype(jnp.int32)


def draw_pair_counts(key, part):
    key = jax.random.fold_in(key, 23)
    first_key, second_key = jax.random.split(key)
    grid_shape = (N_ROW * STEPS, N_COL)
    drawn = jax.random.randint(first_key, grid_shape, PAIRS // 2, PAIRS + 1)
    picked = jax.random.randint(second_key, (STEPS,), 0, N_ROW * N_COL)
    row_index = lax.broadcasted_iota(jnp.int32, grid_shape, 0)
    column_index = lax.broadcasted_iota(jnp.int32, grid_shape, 1)
    device_index = row_index // STEPS * N_COL + column_index
    chosen = picked[row_index % STEPS]
    return jnp.where(device_index == chosen, PAIRS, drawn).astype(jnp.int32)


def steps_of(stream_key, shape, pieces, low, largest):
    def one(position, parts):
        heights = jax.random.uniform(jax.random.fold_in(jax.random.fold_in(stream_key, 6), position), (parts,), jnp.float32, low / len(pieces), largest / len(pieces))
        return jnp.repeat(jnp.exp(heights), shape[position] // parts).reshape((-1,) + (1,) * (len(shape) - position - 1))

    loudness = one(*pieces[0])
    for cut in pieces[1:]:
        loudness = loudness * one(*cut)
    return loudness


def noise(stream_key, extent, deviation, limit, shards=(), held_as=jnp.bfloat16):
    entries = jax.random.normal(stream_key, extent, jnp.float32) * deviation
    if len(shards) > 0:
        entries = steps_of(stream_key, extent, shards, -0.22, 0.18) * entries
    return jnp.clip(entries, min=-limit, max=limit).astype(held_as)


def setup_inputs(seed: int = 0, part: int = 0) -> dict:
    streams_of = jax.random.split(jax.random.key(seed), 5)
    part_keys = jax.random.split(jax.random.fold_in(streams_of[4], part), 5)
    p_tiles = noise(part_keys[0], (N_ROW * CAPA, N_COL * BLK, BLK), BLK ** -0.5, 0.5, ((0, 4), (1, 4)), jnp.float32)
    h_tiles = noise(part_keys[1], (N_ROW * CAPB, N_COL * BLK, BLK), 1.0, 6.0, ((0, 4), (1, 4)), jnp.float32)
    pair_lists = draw_pair_lists(jax.random.fold_in(jax.random.fold_in(streams_of[4], part), 71), part)
    pair_counts = draw_pair_counts(jax.random.fold_in(jax.random.fold_in(streams_of[4], part), 71), part)
    return dict(p_tiles=p_tiles, h_tiles=h_tiles, pair_lists=pair_lists, pair_counts=pair_counts)


def stack_products(panel_tile, slab_tile, triples, live_count, accum):
    live_mask = jnp.arange(triples.shape[1]) < live_count
    left_blocks = jnp.take(panel_tile, triples[0], axis=0)
    right_blocks = jnp.take(slab_tile, triples[1], axis=0)
    products = jnp.einsum("pij,pjk->pik", left_blocks, right_blocks, precision=lax.Precision.HIGHEST)
    products = jnp.where(live_mask[:, None, None], products, jnp.zeros_like(products))
    return accum + jax.ops.segment_sum(products, triples[2], num_segments=accum.shape[0])


def reference(p_tiles, h_tiles, pair_lists, pair_counts):
    panels = p_tiles.reshape(N_ROW, CAPA, N_COL, BLK, BLK).transpose(0, 2, 1, 3, 4)
    slabs = h_tiles.reshape(N_ROW, CAPB, N_COL, BLK, BLK).transpose(0, 2, 1, 3, 4)
    triples_all = pair_lists.reshape(N_ROW, STEPS, 3, N_COL, PAIRS).transpose(0, 3, 1, 2, 4)
    counts_all = pair_counts.reshape(N_ROW, STEPS, N_COL).transpose(0, 2, 1)
    devices = N_ROW * N_COL
    accum = jnp.zeros((devices, CAPC, BLK, BLK), p_tiles.dtype)
    for step_index in range(STEPS):
        moved_panels = jnp.roll(panels, -step_index, axis=1).reshape(devices, CAPA, BLK, BLK)
        moved_slabs = jnp.roll(slabs, -step_index, axis=0).reshape(devices, CAPB, BLK, BLK)
        step_triples = triples_all[:, :, step_index].reshape(devices, 3, PAIRS)
        step_counts = counts_all[:, :, step_index].reshape(devices)

        def one_tile(items):
            return stack_products(items[0], items[1], items[2], items[3], items[4])

        accum = lax.map(one_tile, (moved_panels, moved_slabs, step_triples, step_counts, accum))
    result = accum.reshape(N_ROW, N_COL, CAPC, BLK, BLK).transpose(0, 2, 1, 3, 4)
    return result.reshape(N_ROW * CAPC, N_COL * BLK, BLK)
```

```python
import functools

import jax
import jax.numpy as jnp
from jax import lax
from jax.experimental import pallas as pl
from jax.experimental.pallas import tpu as pltpu
from jax.sharding import PartitionSpec as P

STEPS = 4
CAPC = 48
GROUP = 4


def from_behind(value, axis, steps):
    count = lax.axis_size(axis)
    pairs = [(source, (source + steps) % count) for source in range(count)]
    return lax.ppermute(value, axis, pairs)


def split(value):
    high = value.astype(jnp.bfloat16)
    low = (value - high.astype(jnp.float32)).astype(jnp.bfloat16)
    return high, low


def split_left(source, target, first, count):
    def body(slot, carry):
        high, low = split(source[slot])
        target[slot, :, 0:128] = high
        target[slot, :, 128:256] = low
        return carry

    lax.fori_loop(first, first + count, body, 0)


def split_right(source, target, first, count):
    def body(slot, carry):
        high, low = split(source[slot])
        target[slot, 0:128, 0:128] = high
        target[slot, 0:128, 128:256] = low
        target[slot, 128:256, 0:128] = high
        return carry

    lax.fori_loop(first, first + count, body, 0)


def clear_corner(target, count):
    def body(slot, carry):
        target[slot, 128:256, 128:256] = jnp.zeros((128, 128), jnp.bfloat16)
        return carry

    lax.fori_loop(0, count, body, 0)


def multiply(left, right):
    both = jnp.dot(left, right, preferred_element_type=jnp.float32)
    return both[:, 0:128] + both[:, 128:256]


def step_kernel(lists, live, left, right, before, after, left_parts, right_parts):
    split_left(left, left_parts, 0, left.shape[0])
    clear_corner(right_parts, right.shape[0])
    split_right(right, right_parts, 0, right.shape[0])
    after[...] = before[...]
    count = live[0]

    def body(group, carry):
        first = group * GROUP
        products = []
        for k in range(GROUP):
            product = multiply(left_parts[lists[0, first + k]], right_parts[lists[1, first + k]])
            products.append(jnp.where(first + k < count, product, 0.0))
        for k in range(GROUP):
            place = lists[2, first + k]
            after[place] = after[place] + products[k]
        return carry

    lax.fori_loop(0, (count + GROUP - 1) // GROUP, body, 0)


def step(left, right, lists, live, before):
    width = lists.shape[1]
    return pl.pallas_call(
        step_kernel,
        out_shape=jax.ShapeDtypeStruct(before.shape, jnp.float32),
        in_specs=[
            pl.BlockSpec(memory_space=pltpu.SMEM),
            pl.BlockSpec(memory_space=pltpu.SMEM),
            pl.BlockSpec(memory_space=pltpu.VMEM),
            pl.BlockSpec(memory_space=pltpu.VMEM),
            pl.BlockSpec(memory_space=pltpu.VMEM),
        ],
        out_specs=pl.BlockSpec(memory_space=pltpu.VMEM),
        scratch_shapes=[
            pltpu.VMEM((left.shape[0], 128, 256), jnp.bfloat16),
            pltpu.VMEM((right.shape[0], 256, 256), jnp.bfloat16),
        ],
        compiler_params=pltpu.CompilerParams(vmem_limit_bytes=40 << 20),
        cost_estimate=pl.CostEstimate(
            flops=width * 2 * 128 * 256 * 256, bytes_accessed=12 << 20, transcendentals=0
        ),
    )(lists, live, left, right, before)


def shards(p_tiles, h_tiles, pair_lists, pair_counts):
    accum = jnp.zeros((CAPC, p_tiles.shape[1], p_tiles.shape[2]), jnp.float32)
    panel_tile = p_tiles
    slab_tile = h_tiles
    for index in range(STEPS):
        if index > 0:
            panel_tile = from_behind(panel_tile, "col", -1)
            slab_tile = from_behind(slab_tile, "row", -1)
        lists = pair_lists[3 * index : 3 * index + 3]
        accum = step(panel_tile, slab_tile, lists, pair_counts[index], accum)
    return accum


def solution(mesh):
    placed = (
        P(("groups", "row"), "col", None),
        P(("groups", "row"), "col", None),
        P(("groups", "row"), "col"),
        P(("groups", "row"), "col"),
    )
    return jax.shard_map(
        shards,
        mesh=mesh,
        in_specs=placed,
        out_specs=P(("groups", "row"), "col", None),
        check_vma=False,
    )
```

```python
import functools

import jax
import jax.numpy as jnp
from jax import lax
from jax.experimental import pallas as pl
from jax.experimental.pallas import tpu as pltpu
from jax.sharding import PartitionSpec as P

STEPS = 4
CAPC = 48
GROUP = 4


def from_behind(value, axis, steps):
    count = lax.axis_size(axis)
    pairs = [(source, (source + steps) % count) for source in range(count)]
    return lax.ppermute(value, axis, pairs)


def split(value):
    high = value.astype(jnp.bfloat16)
    low = (value - high.astype(jnp.float32)).astype(jnp.bfloat16)
    return high, low


def split_left(source, target, first, count):
    def body(slot, carry):
        high, low = split(source[slot])
        target[slot, :, 0:128] = high
        target[slot, :, 128:256] = low
        return carry

    lax.fori_loop(first, first + count, body, 0)


def split_right(source, target, first, count):
    def body(slot, carry):
        high, low = split(source[slot])
        target[slot, 0:128, 0:128] = high
        target[slot, 0:128, 128:256] = low
        target[slot, 128:256, 0:128] = high
        return carry

    lax.fori_loop(first, first + count, body, 0)


def clear_corner(target, count):
    def body(slot, carry):
        target[slot, 128:256, 128:256] = jnp.zeros((128, 128), jnp.bfloat16)
        return carry

    lax.fori_loop(0, count, body, 0)


def multiply(left, right):
    both = jnp.dot(left, right, preferred_element_type=jnp.float32)
    return both[:, 0:128] + both[:, 128:256]


def step_kernel(lists, live, left, right, before, after, left_parts, right_parts):
    split_left(left, left_parts, 0, left.shape[0])
    clear_corner(right_parts, right.shape[0])
    split_right(right, right_parts, 0, right.shape[0])
    after[...] = before[...]
    count = live[0]

    def body(group, carry):
        first = group * GROUP
        products = []
        for k in range(GROUP):
            product = multiply(left_parts[lists[0, first + k]], right_parts[lists[1, first + k]])
            products.append(jnp.where(first + k < count, product, 0.0))
        for k in range(GROUP):
            place = lists[2, first + k]
            after[place] = after[place] + products[k]
        return carry

    lax.fori_loop(0, (count + GROUP - 1) // GROUP, body, 0)


def step(left, right, lists, live, before):
    width = lists.shape[1]
    return pl.pallas_call(
        step_kernel,
        out_shape=jax.ShapeDtypeStruct(before.shape, jnp.float32),
        in_specs=[
            pl.BlockSpec(memory_space=pltpu.SMEM),
            pl.BlockSpec(memory_space=pltpu.SMEM),
            pl.BlockSpec(memory_space=pltpu.VMEM),
            pl.BlockSpec(memory_space=pltpu.VMEM),
            pl.BlockSpec(memory_space=pltpu.VMEM),
        ],
        out_specs=pl.BlockSpec(memory_space=pltpu.VMEM),
        scratch_shapes=[
            pltpu.VMEM((left.shape[0], 128, 256), jnp.bfloat16),
            pltpu.VMEM((right.shape[0], 256, 256), jnp.bfloat16),
        ],
        compiler_params=pltpu.CompilerParams(vmem_limit_bytes=40 << 20),
        cost_estimate=pl.CostEstimate(
            flops=width * 2 * 128 * 256 * 256, bytes_accessed=12 << 20, transcendentals=0
        ),
    )(lists, live, left, right, before)


CHUNKS = 4
MESH = pl.DeviceIdType.MESH


def sort_pairs(pair_lists, pair_counts):
    width = pair_lists.shape[1]
    triples = pair_lists.reshape(STEPS, 3, width)
    slot = lax.broadcasted_iota(jnp.int32, (STEPS, width), 1)
    place = jnp.where(slot < pair_counts, triples[:, 2], CAPC)
    order = place * width + slot
    rank = jnp.sum((order[:, None, :] < order[:, :, None]).astype(jnp.int32), axis=2)
    packed = (triples[:, 0] * 1024 + triples[:, 1]) * 1024 + place
    hit = rank[:, :, None] == lax.broadcasted_iota(jnp.int32, (STEPS, width, width), 2)
    ordered = jnp.sum(jnp.where(hit, packed[:, :, None], 0), axis=1)
    target = ordered % 1024
    behind = jnp.concatenate([jnp.full((STEPS, 1), -1, jnp.int32), target[:, :-1]], axis=1)
    keep = (target == behind).astype(jnp.float32)
    kept = lax.broadcasted_iota(jnp.int32, (STEPS, CAPC, width), 1)
    last = jnp.sum((place[:, None, :] <= kept).astype(jnp.int32), axis=2) - 1
    some = jnp.max((place[:, None, :] == kept).astype(jnp.float32), axis=2)
    slots = jnp.concatenate([ordered // 1048576, ordered // 1024 % 1024], axis=0)
    return slots, jnp.maximum(last, 0), keep, some


def ring_kernel(
    slots, last, keep, some, p_ref, h_ref, c_ref,
    panels, slabs, left_parts, right_parts, runs,
    own_sem, p_left, p_right, p_recv, h_send, h_recv,
):
    group = lax.axis_index("groups")
    row = lax.axis_index("row")
    col = lax.axis_index("col")
    count = p_ref.shape[0]
    piece = count // CHUNKS
    width = keep.shape[1]
    sibling = row + 1 - 2 * (row % 2)
    across = (row + 2) % 4
    diagonal = (sibling + 2) % 4

    barrier = pltpu.get_barrier_semaphore()

    def greet(r, c):
        pl.semaphore_signal(barrier, inc=1, device_id=(group, r, c), device_id_type=MESH)

    greet(sibling, col)
    greet(across, col)

    @pl.when(col > 0)
    def _():
        greet(row, col - 1)

    @pl.when(col < 3)
    def _():
        greet(row, col + 1)

    pl.semaphore_wait(barrier, 2 + jnp.minimum(col, 1) + jnp.minimum(3 - col, 1))

    def panel_copy(tile, q, leftward, own=False):
        part = pl.ds(q * piece, piece)
        return pltpu.make_async_remote_copy(
            src_ref=p_ref.at[part] if own else panels.at[tile, part],
            dst_ref=panels.at[tile, part],
            send_sem=p_left.at[tile, q] if leftward else p_right.at[tile, q],
            recv_sem=p_recv.at[tile, q],
            device_id=(group, row, (col + 3) % 4 if leftward else (col + 1) % 4),
            device_id_type=MESH,
        )

    def slab_copy(tile, which, target, own=False):
        return pltpu.make_async_remote_copy(
            src_ref=h_ref if own else slabs.at[tile],
            dst_ref=slabs.at[tile],
            send_sem=h_send.at[which],
            recv_sem=h_recv.at[tile],
            device_id=(group, target, col),
            device_id_type=MESH,
        )

    for q in range(CHUNKS):
        @pl.when(col > 0)
        def _():
            panel_copy(col, q, True, True).start()

        @pl.when(col < 3)
        def _():
            panel_copy(col, q, False, True).start()

    slab_copy(row, 0, across, True).start()
    slab_copy(row, 1, sibling, True).start()
    own_panel = pltpu.make_async_copy(p_ref, panels.at[col], own_sem.at[0])
    own_slab = pltpu.make_async_copy(h_ref, slabs.at[row], own_sem.at[1])
    own_panel.start()
    own_slab.start()
    clear_corner(right_parts, h_ref.shape[0])
    own_panel.wait()
    own_slab.wait()

    def products(index, first):
        def body(block, acc):
            start = block * GROUP
            found = []
            for k in range(GROUP):
                found.append(
                    multiply(
                        left_parts[slots[index, start + k]],
                        right_parts[slots[STEPS + index, start + k]],
                    )
                )
            for k in range(GROUP):
                acc = acc * keep[index, start + k] + found[k]
                runs[start + k] = acc
            return acc

        lax.fori_loop(0, width // GROUP, body, jnp.zeros((128, 128), jnp.float32))

        def collect(j, carry):
            term = runs[last[index, j]] * some[index, j]
            c_ref[j] = term if first else c_ref[j] + term
            return carry

        lax.fori_loop(0, c_ref.shape[0], collect, 0)

    def take(distance, q):
        @pl.when(col + distance <= 3)
        def _():
            panel_copy(col + distance, q, True).wait_recv()

            @pl.when(col > 0)
            def _():
                panel_copy(col + distance, q, True).start()

        @pl.when(col - distance >= 0)
        def _():
            panel_copy(col - distance, q, False).wait_recv()

            @pl.when(col < 3)
            def _():
                panel_copy(col - distance, q, False).start()

    split_left(panels.at[col], left_parts, 0, count)
    split_right(slabs.at[row], right_parts, 0, h_ref.shape[0])
    products(0, True)
    for distance in (1, 2):
        for q in range(CHUNKS):
            take(distance, q)
    slab_copy(sibling, 1, sibling).wait_recv()
    slab_copy(across, 0, across).wait_recv()
    slab_copy(across, 2, sibling).start()
    slab_copy(diagonal, 2, sibling).wait_recv()
    for i in range(1, STEPS):
        index = jnp.where(col < 2, i, STEPS - i)
        split_right(slabs.at[(row + index) % 4], right_parts, 0, h_ref.shape[0])
        for q in range(CHUNKS):
            if i == 3:
                take(3, q)
            split_left(panels.at[(col + index) % 4], left_parts, q * piece, piece)
        products(index, False)

    for tile in range(4):
        for q in range(CHUNKS):
            @pl.when(jnp.logical_and(col > 0, tile >= col))
            def _():
                panel_copy(tile, q, True).wait_send()

            @pl.when(jnp.logical_and(col < 3, tile <= col))
            def _():
                panel_copy(tile, q, False).wait_send()

    slab_copy(row, 0, across).wait_send()
    slab_copy(row, 1, sibling).wait_send()
    slab_copy(across, 2, sibling).wait_send()


def ring(p_tiles, h_tiles, pair_lists, pair_counts):
    slots, last, keep, some = sort_pairs(pair_lists, pair_counts)
    count, slabs = p_tiles.shape[0], h_tiles.shape[0]
    dma = pltpu.SemaphoreType.DMA
    return pl.pallas_call(
        ring_kernel,
        out_shape=jax.ShapeDtypeStruct((CAPC, 128, 128), jnp.float32),
        in_specs=[pl.BlockSpec(memory_space=pltpu.SMEM)] * 4
        + [pl.BlockSpec(memory_space=pl.ANY)] * 2,
        out_specs=pl.BlockSpec(memory_space=pltpu.VMEM),
        scratch_shapes=[
            pltpu.VMEM((4, count, 128, 128), jnp.float32),
            pltpu.VMEM((4, slabs, 128, 128), jnp.float32),
            pltpu.VMEM((count, 128, 256), jnp.bfloat16),
            pltpu.VMEM((slabs, 256, 256), jnp.bfloat16),
            pltpu.VMEM((pair_lists.shape[1], 128, 128), jnp.float32),
            dma((2,)),
            dma((4, CHUNKS)),
            dma((4, CHUNKS)),
            dma((4, CHUNKS)),
            dma((3,)),
            dma((4,)),
        ],
        compiler_params=pltpu.CompilerParams(
            collective_id=0, has_side_effects=True, vmem_limit_bytes=48 << 20
        ),
        cost_estimate=pl.CostEstimate(
            flops=STEPS * 96 * 2 * 128 * 256 * 256, bytes_accessed=12 << 20, transcendentals=0
        ),
    )(slots, last, keep, some, p_tiles, h_tiles)


def shards(p_tiles, h_tiles, pair_lists, pair_counts):
    if lax.axis_size("row") == 4 and lax.axis_size("col") == 4:
        return ring(p_tiles, h_tiles, pair_lists, pair_counts)
    accum = jnp.zeros((CAPC, p_tiles.shape[1], p_tiles.shape[2]), jnp.float32)
    panel_tile = p_tiles
    slab_tile = h_tiles
    for index in range(STEPS):
        if index > 0:
            panel_tile = from_behind(panel_tile, "col", -1)
            slab_tile = from_behind(slab_tile, "row", -1)
        lists = pair_lists[3 * index : 3 * index + 3]
        accum = step(panel_tile, slab_tile, lists, pair_counts[index], accum)
    return accum


def solution(mesh):
    placed = (
        P(("groups", "row"), "col", None),
        P(("groups", "row"), "col", None),
        P(("groups", "row"), "col"),
        P(("groups", "row"), "col"),
    )
    return jax.shard_map(
        shards,
        mesh=mesh,
        in_specs=placed,
        out_specs=P(("groups", "row"), "col", None),
        check_vma=False,
    )
```

```python
import functools

import jax
import jax.numpy as jnp
from jax import lax
from jax.experimental import pallas as pl
from jax.experimental.pallas import tpu as pltpu
from jax.sharding import PartitionSpec as P

STEPS = 4
CAPC = 48
GROUP = 4


def from_behind(value, axis, steps):
    count = lax.axis_size(axis)
    pairs = [(source, (source + steps) % count) for source in range(count)]
    return lax.ppermute(value, axis, pairs)


def split(value):
    high = value.astype(jnp.bfloat16)
    low = (value - high.astype(jnp.float32)).astype(jnp.bfloat16)
    return high, low


def split_left(source, target, first, rows):
    part = pl.ds(first, rows)

    def body(slot, carry):
        high, low = split(source[slot, part, :])
        target[slot, part, 0:128] = high
        target[slot, part, 128:256] = low
        return carry

    lax.fori_loop(0, source.shape[0], body, 0)


def split_right(source, target, first, count):
    def body(slot, carry):
        high, low = split(source[slot])
        target[slot, 0:128, 0:128] = high
        target[slot, 0:128, 128:256] = low
        target[slot, 128:256, 0:128] = high
        return carry

    lax.fori_loop(first, first + count, body, 0)


def clear_corner(target, count):
    def body(slot, carry):
        target[slot, 128:256, 128:256] = jnp.zeros((128, 128), jnp.bfloat16)
        return carry

    lax.fori_loop(0, count, body, 0)


def multiply(left, right):
    both = jnp.dot(left, right, preferred_element_type=jnp.float32)
    return both[:, 0:128] + both[:, 128:256]


def step_kernel(lists, live, left, right, before, after, left_parts, right_parts):
    split_left(left, left_parts, 0, left.shape[1])
    clear_corner(right_parts, right.shape[0])
    split_right(right, right_parts, 0, right.shape[0])
    after[...] = before[...]
    count = live[0]

    def body(group, carry):
        first = group * GROUP
        products = []
        for k in range(GROUP):
            product = multiply(left_parts[lists[0, first + k]], right_parts[lists[1, first + k]])
            products.append(jnp.where(first + k < count, product, 0.0))
        for k in range(GROUP):
            place = lists[2, first + k]
            after[place] = after[place] + products[k]
        return carry

    lax.fori_loop(0, (count + GROUP - 1) // GROUP, body, 0)


def step(left, right, lists, live, before):
    width = lists.shape[1]
    return pl.pallas_call(
        step_kernel,
        out_shape=jax.ShapeDtypeStruct(before.shape, jnp.float32),
        in_specs=[
            pl.BlockSpec(memory_space=pltpu.SMEM),
            pl.BlockSpec(memory_space=pltpu.SMEM),
            pl.BlockSpec(memory_space=pltpu.VMEM),
            pl.BlockSpec(memory_space=pltpu.VMEM),
            pl.BlockSpec(memory_space=pltpu.VMEM),
        ],
        out_specs=pl.BlockSpec(memory_space=pltpu.VMEM),
        scratch_shapes=[
            pltpu.VMEM((left.shape[0], 128, 256), jnp.bfloat16),
            pltpu.VMEM((right.shape[0], 256, 256), jnp.bfloat16),
        ],
        compiler_params=pltpu.CompilerParams(vmem_limit_bytes=40 << 20),
        cost_estimate=pl.CostEstimate(
            flops=width * 2 * 128 * 256 * 256, bytes_accessed=12 << 20, transcendentals=0
        ),
    )(lists, live, left, right, before)


CHUNKS = 4
MESH = pl.DeviceIdType.MESH


def sort_pairs(pair_lists, pair_counts):
    width = pair_lists.shape[1]
    triples = pair_lists.reshape(STEPS, 3, width)
    slot = lax.broadcasted_iota(jnp.int32, (STEPS, width), 1)
    place = jnp.where(slot < pair_counts, triples[:, 2], CAPC)
    order = place * width + slot
    rank = jnp.sum((order[:, None, :] < order[:, :, None]).astype(jnp.int32), axis=2)
    packed = (triples[:, 0] * 1024 + triples[:, 1]) * 1024 + place
    hit = rank[:, :, None] == lax.broadcasted_iota(jnp.int32, (STEPS, width, width), 2)
    ordered = jnp.sum(jnp.where(hit, packed[:, :, None], 0), axis=1)
    target = ordered % 1024
    behind = jnp.concatenate([jnp.full((STEPS, 1), -1, jnp.int32), target[:, :-1]], axis=1)
    keep = (target == behind).astype(jnp.float32)
    kept = lax.broadcasted_iota(jnp.int32, (STEPS, CAPC, width), 1)
    last = jnp.sum((place[:, None, :] <= kept).astype(jnp.int32), axis=2) - 1
    some = jnp.max((place[:, None, :] == kept).astype(jnp.float32), axis=2)
    slots = jnp.concatenate([ordered // 1048576, ordered // 1024 % 1024], axis=0)
    return slots, jnp.maximum(last, 0), keep, some


def ring_kernel(
    slots, last, keep, some, p_ref, h_ref, out_ref,
    c_ref, panels, slabs, left_parts, right_parts, runs,
    own_sem, out_sem, p_left, p_right, p_recv, h_send, h_recv,
):
    group = lax.axis_index("groups")
    row = lax.axis_index("row")
    col = lax.axis_index("col")
    piece = p_ref.shape[1] // CHUNKS
    width = keep.shape[1]
    sibling = row + 1 - 2 * (row % 2)
    across = (row + 2) % 4
    diagonal = (sibling + 2) % 4

    barrier = pltpu.get_barrier_semaphore()

    def greet(r, c):
        pl.semaphore_signal(barrier, inc=1, device_id=(group, r, c), device_id_type=MESH)

    greet(sibling, col)
    greet(across, col)

    @pl.when(col > 0)
    def _():
        greet(row, col - 1)

    @pl.when(col < 3)
    def _():
        greet(row, col + 1)

    pl.semaphore_wait(barrier, 2 + jnp.minimum(col, 1) + jnp.minimum(3 - col, 1))

    def panel_copy(tile, q, leftward, own=False):
        part = pl.ds(q * piece, piece)
        return pltpu.make_async_remote_copy(
            src_ref=p_ref.at[:, part] if own else panels.at[tile, :, part],
            dst_ref=panels.at[tile, :, part],
            send_sem=p_left.at[tile, q] if leftward else p_right.at[tile, q],
            recv_sem=p_recv.at[tile, q],
            device_id=(group, row, (col + 3) % 4 if leftward else (col + 1) % 4),
            device_id_type=MESH,
        )

    def slab_copy(tile, which, target, own=False):
        return pltpu.make_async_remote_copy(
            src_ref=h_ref if own else slabs.at[tile],
            dst_ref=slabs.at[tile],
            send_sem=h_send.at[which],
            recv_sem=h_recv.at[tile],
            device_id=(group, target, col),
            device_id_type=MESH,
        )

    for q in range(CHUNKS):
        @pl.when(col > 0)
        def _():
            panel_copy(col, q, True, True).start()

        @pl.when(col < 3)
        def _():
            panel_copy(col, q, False, True).start()

    slab_copy(row, 0, across, True).start()
    slab_copy(row, 1, sibling, True).start()
    own_panel = pltpu.make_async_copy(p_ref, panels.at[col], own_sem.at[0])
    own_slab = pltpu.make_async_copy(h_ref, slabs.at[row], own_sem.at[1])
    own_panel.start()
    own_slab.start()
    clear_corner(right_parts, h_ref.shape[0])
    own_panel.wait()
    own_slab.wait()

    def products(index, first, low, rows):
        part = pl.ds(low, rows)

        def body(block, acc):
            start = block * GROUP
            found = []
            for k in range(GROUP):
                found.append(
                    multiply(
                        left_parts[slots[index, start + k], part, :],
                        right_parts[slots[STEPS + index, start + k]],
                    )
                )
            for k in range(GROUP):
                acc = acc * keep[index, start + k] + found[k]
                runs[start + k, part, :] = acc
            return acc

        lax.fori_loop(0, width // GROUP, body, jnp.zeros((rows, 128), jnp.float32))

        def collect(j, carry):
            term = runs[last[index, j], part, :] * some[index, j]
            c_ref[j, part, :] = term if first else c_ref[j, part, :] + term
            return carry

        lax.fori_loop(0, c_ref.shape[0], collect, 0)

    def out_copy(low, rows, which):
        part = pl.ds(low, rows)
        return pltpu.make_async_copy(c_ref.at[:, part], out_ref.at[:, part], out_sem.at[which])

    def take(distance, q):
        @pl.when(col + distance <= 3)
        def _():
            panel_copy(col + distance, q, True).wait_recv()

            @pl.when(col > 0)
            def _():
                panel_copy(col + distance, q, True).start()

        @pl.when(col - distance >= 0)
        def _():
            panel_copy(col - distance, q, False).wait_recv()

            @pl.when(col < 3)
            def _():
                panel_copy(col - distance, q, False).start()

    split_left(panels.at[col], left_parts, 0, 128)
    split_right(slabs.at[row], right_parts, 0, h_ref.shape[0])
    products(0, True, 0, 128)
    for distance in (1, 2):
        for q in range(CHUNKS):
            take(distance, q)
    slab_copy(sibling, 1, sibling).wait_recv()
    slab_copy(across, 0, across).wait_recv()
    slab_copy(across, 2, sibling).start()
    slab_copy(diagonal, 2, sibling).wait_recv()
    for i in range(1, STEPS):
        index = jnp.where(col < 2, i, STEPS - i)
        split_right(slabs.at[(row + index) % 4], right_parts, 0, h_ref.shape[0])
        left = panels.at[(col + index) % 4]
        if i < STEPS - 1:
            split_left(left, left_parts, 0, 128)
            products(index, False, 0, 128)
            continue
        for q in range(CHUNKS - 1):
            take(3, q)
        early = 128 - piece
        split_left(left, left_parts, 0, early)
        products(index, False, 0, early)
        out_copy(0, early, 0).start()
        take(3, CHUNKS - 1)
        split_left(left, left_parts, early, piece)
        products(index, False, early, piece)
        out_copy(early, piece, 1).start()
        out_copy(0, early, 0).wait()
        out_copy(early, piece, 1).wait()

    for tile in range(4):
        for q in range(CHUNKS):
            @pl.when(jnp.logical_and(col > 0, tile >= col))
            def _():
                panel_copy(tile, q, True).wait_send()

            @pl.when(jnp.logical_and(col < 3, tile <= col))
            def _():
                panel_copy(tile, q, False).wait_send()

    slab_copy(row, 0, across).wait_send()
    slab_copy(row, 1, sibling).wait_send()
    slab_copy(across, 2, sibling).wait_send()


def ring(p_tiles, h_tiles, pair_lists, pair_counts):
    slots, last, keep, some = sort_pairs(pair_lists, pair_counts)
    count, slabs = p_tiles.shape[0], h_tiles.shape[0]
    dma = pltpu.SemaphoreType.DMA
    return pl.pallas_call(
        ring_kernel,
        out_shape=jax.ShapeDtypeStruct((CAPC, 128, 128), jnp.float32),
        in_specs=[pl.BlockSpec(memory_space=pltpu.SMEM)] * 4
        + [pl.BlockSpec(memory_space=pl.ANY)] * 2,
        out_specs=pl.BlockSpec(memory_space=pl.ANY),
        scratch_shapes=[
            pltpu.VMEM((CAPC, 128, 128), jnp.float32),
            pltpu.VMEM((4, count, 128, 128), jnp.float32),
            pltpu.VMEM((4, slabs, 128, 128), jnp.float32),
            pltpu.VMEM((count, 128, 256), jnp.bfloat16),
            pltpu.VMEM((slabs, 256, 256), jnp.bfloat16),
            pltpu.VMEM((pair_lists.shape[1], 128, 128), jnp.float32),
            dma((2,)),
            dma((2,)),
            dma((4, CHUNKS)),
            dma((4, CHUNKS)),
            dma((4, CHUNKS)),
            dma((3,)),
            dma((4,)),
        ],
        compiler_params=pltpu.CompilerParams(
            collective_id=0, has_side_effects=True, vmem_limit_bytes=48 << 20
        ),
        cost_estimate=pl.CostEstimate(
            flops=STEPS * 96 * 2 * 128 * 256 * 256, bytes_accessed=12 << 20, transcendentals=0
        ),
    )(slots, last, keep, some, p_tiles, h_tiles)


def shards(p_tiles, h_tiles, pair_lists, pair_counts):
    if lax.axis_size("row") == 4 and lax.axis_size("col") == 4:
        return ring(p_tiles, h_tiles, pair_lists, pair_counts)
    accum = jnp.zeros((CAPC, p_tiles.shape[1], p_tiles.shape[2]), jnp.float32)
    panel_tile = p_tiles
    slab_tile = h_tiles
    for index in range(STEPS):
        if index > 0:
            panel_tile = from_behind(panel_tile, "col", -1)
            slab_tile = from_behind(slab_tile, "row", -1)
        lists = pair_lists[3 * index : 3 * index + 3]
        accum = step(panel_tile, slab_tile, lists, pair_counts[index], accum)
    return accum


def solution(mesh):
    placed = (
        P(("groups", "row"), "col", None),
        P(("groups", "row"), "col", None),
        P(("groups", "row"), "col"),
        P(("groups", "row"), "col"),
    )
    return jax.shard_map(
        shards,
        mesh=mesh,
        in_specs=placed,
        out_specs=P(("groups", "row"), "col", None),
        check_vma=False,
    )
```

```python
import functools

import jax
import jax.numpy as jnp
from jax import lax
from jax.experimental import pallas as pl
from jax.experimental.pallas import tpu as pltpu
from jax.sharding import PartitionSpec as P

STEPS = 4
CAPC = 48
GROUP = 4


def from_behind(value, axis, steps):
    count = lax.axis_size(axis)
    pairs = [(source, (source + steps) % count) for source in range(count)]
    return lax.ppermute(value, axis, pairs)


def split(value):
    high = value.astype(jnp.bfloat16)
    low = (value - high.astype(jnp.float32)).astype(jnp.bfloat16)
    return high, low


def split_left(source, target, first, rows):
    part = pl.ds(first, rows)

    def body(slot, carry):
        high, low = split(source[slot, part, :])
        target[slot, part, 0:128] = high
        target[slot, part, 128:256] = low
        return carry

    lax.fori_loop(0, source.shape[0], body, 0)


def split_right(source, target, first, count):
    def body(slot, carry):
        high, low = split(source[slot])
        target[slot, 0:128, 0:128] = high
        target[slot, 0:128, 128:256] = low
        target[slot, 128:256, 0:128] = high
        return carry

    lax.fori_loop(first, first + count, body, 0)


def clear_corner(target, count):
    def body(slot, carry):
        target[slot, 128:256, 128:256] = jnp.zeros((128, 128), jnp.bfloat16)
        return carry

    lax.fori_loop(0, count, body, 0)


def multiply(left, right):
    both = jnp.dot(left, right, preferred_element_type=jnp.float32)
    return both[:, 0:128] + both[:, 128:256]


def step_kernel(lists, live, left, right, before, after, left_parts, right_parts):
    split_left(left, left_parts, 0, left.shape[1])
    clear_corner(right_parts, right.shape[0])
    split_right(right, right_parts, 0, right.shape[0])
    after[...] = before[...]
    count = live[0]

    def body(group, carry):
        first = group * GROUP
        products = []
        for k in range(GROUP):
            product = multiply(left_parts[lists[0, first + k]], right_parts[lists[1, first + k]])
            products.append(jnp.where(first + k < count, product, 0.0))
        for k in range(GROUP):
            place = lists[2, first + k]
            after[place] = after[place] + products[k]
        return carry

    lax.fori_loop(0, (count + GROUP - 1) // GROUP, body, 0)


def step(left, right, lists, live, before):
    width = lists.shape[1]
    return pl.pallas_call(
        step_kernel,
        out_shape=jax.ShapeDtypeStruct(before.shape, jnp.float32),
        in_specs=[
            pl.BlockSpec(memory_space=pltpu.SMEM),
            pl.BlockSpec(memory_space=pltpu.SMEM),
            pl.BlockSpec(memory_space=pltpu.VMEM),
            pl.BlockSpec(memory_space=pltpu.VMEM),
            pl.BlockSpec(memory_space=pltpu.VMEM),
        ],
        out_specs=pl.BlockSpec(memory_space=pltpu.VMEM),
        scratch_shapes=[
            pltpu.VMEM((left.shape[0], 128, 256), jnp.bfloat16),
            pltpu.VMEM((right.shape[0], 256, 256), jnp.bfloat16),
        ],
        compiler_params=pltpu.CompilerParams(vmem_limit_bytes=40 << 20),
        cost_estimate=pl.CostEstimate(
            flops=width * 2 * 128 * 256 * 256, bytes_accessed=12 << 20, transcendentals=0
        ),
    )(lists, live, left, right, before)


CHUNKS = 4
MESH = pl.DeviceIdType.MESH


def sort_pairs(lists, count, index, table):
    width = lists.shape[1]
    lane = lax.broadcasted_iota(jnp.int32, (width, width), 1)
    diagonal = lax.broadcasted_iota(jnp.int32, (width, width), 0) == lane
    slot = lax.broadcasted_iota(jnp.int32, (1, width), 1)

    def column(line):
        return jnp.sum(jnp.where(diagonal, line, 0), axis=1, keepdims=True)

    def total(mask, values):
        return jnp.sum(jnp.where(mask, values, 0), axis=0, keepdims=True)

    triple = [lists[3 * index + role : 3 * index + role + 1, :] for role in range(3)]
    place = jnp.where(slot < count, triple[2], CAPC)
    order = place * width + slot
    rank = jnp.sum((order < column(order)).astype(jnp.int32), axis=1, keepdims=True)
    place_column = column(place)
    hit = rank == lane
    target = total(hit, place_column)
    behind = jnp.where(slot == 0, -1, total(rank == lane - 1, place_column))
    lines = (
        total(hit, column(triple[0])),
        total(hit, column(triple[1])),
        (target == behind).astype(jnp.int32),
        jnp.maximum(total(place_column <= lane, 1) - 1, 0),
        jnp.minimum(total(place_column == lane, 1), 1),
    )
    for role, line in enumerate(lines):
        table[8 * index + role : 8 * index + role + 1, 0:width] = line


def ring_kernel(
    live, lists_ref, p_ref, h_ref, out_ref,
    lists, table, slots, c_ref, panels, slabs, left_parts, right_parts, runs,
    own_sem, out_sem, p_left, p_right, p_recv, h_send, h_recv,
):
    group = lax.axis_index("groups")
    row = lax.axis_index("row")
    col = lax.axis_index("col")
    piece = p_ref.shape[1] // CHUNKS
    width = lists_ref.shape[1]
    sibling = row + 1 - 2 * (row % 2)
    across = (row + 2) % 4
    diagonal = (sibling + 2) % 4

    barrier = pltpu.get_barrier_semaphore()

    def greet(r, c):
        pl.semaphore_signal(barrier, inc=1, device_id=(group, r, c), device_id_type=MESH)

    greet(sibling, col)
    greet(across, col)

    @pl.when(col > 0)
    def _():
        greet(row, col - 1)

    @pl.when(col < 3)
    def _():
        greet(row, col + 1)

    pl.semaphore_wait(barrier, 2 + jnp.minimum(col, 1) + jnp.minimum(3 - col, 1))

    def panel_copy(tile, q, leftward, own=False):
        part = pl.ds(q * piece, piece)
        return pltpu.make_async_remote_copy(
            src_ref=p_ref.at[:, part] if own else panels.at[tile, :, part],
            dst_ref=panels.at[tile, :, part],
            send_sem=p_left.at[tile, q] if leftward else p_right.at[tile, q],
            recv_sem=p_recv.at[tile, q],
            device_id=(group, row, (col + 3) % 4 if leftward else (col + 1) % 4),
            device_id_type=MESH,
        )

    def slab_copy(tile, which, target, own=False):
        return pltpu.make_async_remote_copy(
            src_ref=h_ref if own else slabs.at[tile],
            dst_ref=slabs.at[tile],
            send_sem=h_send.at[which],
            recv_sem=h_recv.at[tile],
            device_id=(group, target, col),
            device_id_type=MESH,
        )

    for q in range(CHUNKS):
        @pl.when(col > 0)
        def _():
            panel_copy(col, q, True, True).start()

        @pl.when(col < 3)
        def _():
            panel_copy(col, q, False, True).start()

    slab_copy(row, 0, across, True).start()
    slab_copy(row, 1, sibling, True).start()
    own_lists = pltpu.make_async_copy(lists_ref, lists, own_sem.at[2])
    own_lists.start()
    own_panel = pltpu.make_async_copy(p_ref, panels.at[col], own_sem.at[0])
    own_slab = pltpu.make_async_copy(h_ref, slabs.at[row], own_sem.at[1])
    own_panel.start()
    own_slab.start()
    clear_corner(right_parts, h_ref.shape[0])
    own_lists.wait()
    table[...] = jnp.zeros(table.shape, jnp.int32)
    for index in range(STEPS):
        sort_pairs(lists, live[index, 0], index, table)
    moved = pltpu.make_async_copy(table, slots, own_sem.at[3])
    moved.start()
    moved.wait()
    own_panel.wait()
    own_slab.wait()

    def products(index, first, low, rows):
        part = pl.ds(low, rows)

        def body(block, acc):
            start = block * GROUP
            found = []
            for k in range(GROUP):
                found.append(
                    multiply(
                        left_parts[slots[8 * index, start + k], part, :],
                        right_parts[slots[8 * index + 1, start + k]],
                    )
                )
            for k in range(GROUP):
                acc = acc * slots[8 * index + 2, start + k].astype(jnp.float32) + found[k]
                runs[start + k, part, :] = acc
            return acc

        lax.fori_loop(0, width // GROUP, body, jnp.zeros((rows, 128), jnp.float32))

        def collect(j, carry):
            term = runs[slots[8 * index + 3, j], part, :] * slots[8 * index + 4, j].astype(jnp.float32)
            c_ref[j, part, :] = term if first else c_ref[j, part, :] + term
            return carry

        lax.fori_loop(0, c_ref.shape[0], collect, 0)

    def out_copy(low, rows, which):
        part = pl.ds(low, rows)
        return pltpu.make_async_copy(c_ref.at[:, part], out_ref.at[:, part], out_sem.at[which])

    def take(distance, q):
        @pl.when(col + distance <= 3)
        def _():
            panel_copy(col + distance, q, True).wait_recv()

            @pl.when(col > 0)
            def _():
                panel_copy(col + distance, q, True).start()

        @pl.when(col - distance >= 0)
        def _():
            panel_copy(col - distance, q, False).wait_recv()

            @pl.when(col < 3)
            def _():
                panel_copy(col - distance, q, False).start()

    split_left(panels.at[col], left_parts, 0, 128)
    split_right(slabs.at[row], right_parts, 0, h_ref.shape[0])
    products(0, True, 0, 128)
    for distance in (1, 2):
        for q in range(CHUNKS):
            take(distance, q)
    slab_copy(sibling, 1, sibling).wait_recv()
    slab_copy(across, 0, across).wait_recv()
    slab_copy(across, 2, sibling).start()
    slab_copy(diagonal, 2, sibling).wait_recv()
    for i in range(1, STEPS):
        index = jnp.where(col < 2, i, STEPS - i)
        split_right(slabs.at[(row + index) % 4], right_parts, 0, h_ref.shape[0])
        left = panels.at[(col + index) % 4]
        if i < STEPS - 1:
            split_left(left, left_parts, 0, 128)
            products(index, False, 0, 128)
            continue
        for q in range(CHUNKS - 1):
            take(3, q)
        early = 128 - piece
        split_left(left, left_parts, 0, early)
        products(index, False, 0, early)
        out_copy(0, early, 0).start()
        take(3, CHUNKS - 1)
        split_left(left, left_parts, early, piece)
        products(index, False, early, piece)
        out_copy(early, piece, 1).start()
        out_copy(0, early, 0).wait()
        out_copy(early, piece, 1).wait()

    for tile in range(4):
        for q in range(CHUNKS):
            @pl.when(jnp.logical_and(col > 0, tile >= col))
            def _():
                panel_copy(tile, q, True).wait_send()

            @pl.when(jnp.logical_and(col < 3, tile <= col))
            def _():
                panel_copy(tile, q, False).wait_send()

    slab_copy(row, 0, across).wait_send()
    slab_copy(row, 1, sibling).wait_send()
    slab_copy(across, 2, sibling).wait_send()


def ring(p_tiles, h_tiles, pair_lists, pair_counts):
    count, slabs = p_tiles.shape[0], h_tiles.shape[0]
    dma = pltpu.SemaphoreType.DMA
    return pl.pallas_call(
        ring_kernel,
        out_shape=jax.ShapeDtypeStruct((CAPC, 128, 128), jnp.float32),
        in_specs=[pl.BlockSpec(memory_space=pltpu.SMEM)]
        + [pl.BlockSpec(memory_space=pl.ANY)] * 3,
        out_specs=pl.BlockSpec(memory_space=pl.ANY),
        scratch_shapes=[
            pltpu.VMEM(pair_lists.shape, jnp.int32),
            pltpu.VMEM((8 * STEPS, 128), jnp.int32),
            pltpu.SMEM((8 * STEPS, 128), jnp.int32),
            pltpu.VMEM((CAPC, 128, 128), jnp.float32),
            pltpu.VMEM((4, count, 128, 128), jnp.float32),
            pltpu.VMEM((4, slabs, 128, 128), jnp.float32),
            pltpu.VMEM((count, 128, 256), jnp.bfloat16),
            pltpu.VMEM((slabs, 256, 256), jnp.bfloat16),
            pltpu.VMEM((pair_lists.shape[1], 128, 128), jnp.float32),
            dma((4,)),
            dma((2,)),
            dma((4, CHUNKS)),
            dma((4, CHUNKS)),
            dma((4, CHUNKS)),
            dma((3,)),
            dma((4,)),
        ],
        compiler_params=pltpu.CompilerParams(
            collective_id=0, has_side_effects=True, vmem_limit_bytes=48 << 20
        ),
        cost_estimate=pl.CostEstimate(
            flops=STEPS * 96 * 2 * 128 * 256 * 256, bytes_accessed=12 << 20, transcendentals=0
        ),
    )(pair_counts, pair_lists, p_tiles, h_tiles)


def shards(p_tiles, h_tiles, pair_lists, pair_counts):
    if lax.axis_size("row") == 4 and lax.axis_size("col") == 4:
        return ring(p_tiles, h_tiles, pair_lists, pair_counts)
    accum = jnp.zeros((CAPC, p_tiles.shape[1], p_tiles.shape[2]), jnp.float32)
    panel_tile = p_tiles
    slab_tile = h_tiles
    for index in range(STEPS):
        if index > 0:
            panel_tile = from_behind(panel_tile, "col", -1)
            slab_tile = from_behind(slab_tile, "row", -1)
        lists = pair_lists[3 * index : 3 * index + 3]
        accum = step(panel_tile, slab_tile, lists, pair_counts[index], accum)
    return accum


def solution(mesh):
    placed = (
        P(("groups", "row"), "col", None),
        P(("groups", "row"), "col", None),
        P(("groups", "row"), "col"),
        P(("groups", "row"), "col"),
    )
    return jax.shard_map(
        shards,
        mesh=mesh,
        in_specs=placed,
        out_specs=P(("groups", "row"), "col", None),
        check_vma=False,
    )
```

```python
import functools

import jax
import jax.numpy as jnp
from jax import lax
from jax.experimental import pallas as pl
from jax.experimental.pallas import tpu as pltpu
from jax.sharding import PartitionSpec as P

STEPS = 4
CAPC = 48
GROUP = 4


def from_behind(value, axis, steps):
    count = lax.axis_size(axis)
    pairs = [(source, (source + steps) % count) for source in range(count)]
    return lax.ppermute(value, axis, pairs)


def split(value):
    high = value.astype(jnp.bfloat16)
    low = (value - high.astype(jnp.float32)).astype(jnp.bfloat16)
    return high, low


def split_left(source, target, first, rows):
    part = pl.ds(first, rows)

    def body(slot, carry):
        high, low = split(source[slot, part, :])
        target[slot, part, 0:128] = high
        target[slot, part, 128:256] = low
        return carry

    lax.fori_loop(0, source.shape[0], body, 0)


def split_right(source, target, first, count):
    def body(slot, carry):
        high, low = split(source[slot])
        target[slot, 0:128, 0:128] = high
        target[slot, 0:128, 128:256] = low
        target[slot, 128:256, 0:128] = high
        return carry

    lax.fori_loop(first, first + count, body, 0)


def clear_corner(target, count):
    def body(slot, carry):
        target[slot, 128:256, 128:256] = jnp.zeros((128, 128), jnp.bfloat16)
        return carry

    lax.fori_loop(0, count, body, 0)


def multiply(left, right):
    both = jnp.dot(left, right, preferred_element_type=jnp.float32)
    return both[:, 0:128] + both[:, 128:256]


def step_kernel(lists, live, left, right, before, after, left_parts, right_parts):
    split_left(left, left_parts, 0, left.shape[1])
    clear_corner(right_parts, right.shape[0])
    split_right(right, right_parts, 0, right.shape[0])
    after[...] = before[...]
    count = live[0]

    def body(group, carry):
        first = group * GROUP
        products = []
        for k in range(GROUP):
            product = multiply(left_parts[lists[0, first + k]], right_parts[lists[1, first + k]])
            products.append(jnp.where(first + k < count, product, 0.0))
        for k in range(GROUP):
            place = lists[2, first + k]
            after[place] = after[place] + products[k]
        return carry

    lax.fori_loop(0, (count + GROUP - 1) // GROUP, body, 0)


def step(left, right, lists, live, before):
    width = lists.shape[1]
    return pl.pallas_call(
        step_kernel,
        out_shape=jax.ShapeDtypeStruct(before.shape, jnp.float32),
        in_specs=[
            pl.BlockSpec(memory_space=pltpu.SMEM),
            pl.BlockSpec(memory_space=pltpu.SMEM),
            pl.BlockSpec(memory_space=pltpu.VMEM),
            pl.BlockSpec(memory_space=pltpu.VMEM),
            pl.BlockSpec(memory_space=pltpu.VMEM),
        ],
        out_specs=pl.BlockSpec(memory_space=pltpu.VMEM),
        scratch_shapes=[
            pltpu.VMEM((left.shape[0], 128, 256), jnp.bfloat16),
            pltpu.VMEM((right.shape[0], 256, 256), jnp.bfloat16),
        ],
        compiler_params=pltpu.CompilerParams(vmem_limit_bytes=40 << 20),
        cost_estimate=pl.CostEstimate(
            flops=width * 2 * 128 * 256 * 256, bytes_accessed=12 << 20, transcendentals=0
        ),
    )(lists, live, left, right, before)


CHUNKS = 4
MESH = pl.DeviceIdType.MESH


def sort_pairs(lists, count, index, table):
    width = lists.shape[1]
    lane = lax.broadcasted_iota(jnp.int32, (width, width), 1)
    diagonal = lax.broadcasted_iota(jnp.int32, (width, width), 0) == lane
    slot = lax.broadcasted_iota(jnp.int32, (1, width), 1)

    def column(line):
        return jnp.sum(jnp.where(diagonal, line, 0), axis=1, keepdims=True)

    def total(mask, values):
        return jnp.sum(jnp.where(mask, values, 0), axis=0, keepdims=True)

    triple = [lists[3 * index + role : 3 * index + role + 1, :] for role in range(3)]
    place = jnp.where(slot < count, triple[2], CAPC)
    order = place * width + slot
    rank = jnp.sum((order < column(order)).astype(jnp.int32), axis=1, keepdims=True)
    place_column = column(place)
    hit = rank == lane
    target = total(hit, place_column)
    behind = jnp.where(slot == 0, -1, total(rank == lane - 1, place_column))
    lines = (
        total(hit, column(triple[0])),
        total(hit, column(triple[1])),
        (target == behind).astype(jnp.int32),
        jnp.maximum(total(place_column <= lane, 1) - 1, 0),
        jnp.minimum(total(place_column == lane, 1), 1),
    )
    for role, line in enumerate(lines):
        table[8 * index + role : 8 * index + role + 1, 0:width] = line


def ring_kernel(
    live_ref, lists_ref, p_ref, h_ref, out_ref,
    live, lists, table, slots, c_ref, panels, slabs, left_parts, right_parts, runs,
    own_sem, out_sem, p_left, p_right, p_recv, h_send, h_recv,
):
    group = lax.axis_index("groups")
    row = lax.axis_index("row")
    col = lax.axis_index("col")
    piece = p_ref.shape[1] // CHUNKS
    width = lists_ref.shape[1]
    sibling = row + 1 - 2 * (row % 2)
    across = (row + 2) % 4
    diagonal = (sibling + 2) % 4

    barrier = pltpu.get_barrier_semaphore()

    def greet(r, c):
        pl.semaphore_signal(barrier, inc=1, device_id=(group, r, c), device_id_type=MESH)

    greet(sibling, col)
    greet(across, col)

    @pl.when(col > 0)
    def _():
        greet(row, col - 1)

    @pl.when(col < 3)
    def _():
        greet(row, col + 1)

    pl.semaphore_wait(barrier, 2 + jnp.minimum(col, 1) + jnp.minimum(3 - col, 1))

    def panel_copy(tile, q, leftward, own=False):
        part = pl.ds(q * piece, piece)
        return pltpu.make_async_remote_copy(
            src_ref=p_ref.at[:, part] if own else panels.at[tile, :, part],
            dst_ref=panels.at[tile, :, part],
            send_sem=p_left.at[tile, q] if leftward else p_right.at[tile, q],
            recv_sem=p_recv.at[tile, q],
            device_id=(group, row, (col + 3) % 4 if leftward else (col + 1) % 4),
            device_id_type=MESH,
        )

    def slab_copy(tile, which, target, own=False):
        return pltpu.make_async_remote_copy(
            src_ref=h_ref if own else slabs.at[tile],
            dst_ref=slabs.at[tile],
            send_sem=h_send.at[which],
            recv_sem=h_recv.at[tile],
            device_id=(group, target, col),
            device_id_type=MESH,
        )

    for q in range(CHUNKS):
        @pl.when(col > 0)
        def _():
            panel_copy(col, q, True, True).start()

        @pl.when(col < 3)
        def _():
            panel_copy(col, q, False, True).start()

    slab_copy(row, 0, across, True).start()
    slab_copy(row, 1, sibling, True).start()
    own_lists = pltpu.make_async_copy(lists_ref, lists, own_sem.at[2])
    own_lists.start()
    own_live = pltpu.make_async_copy(live_ref, live, own_sem.at[4])
    own_live.start()
    own_panel = pltpu.make_async_copy(p_ref, panels.at[col], own_sem.at[0])
    own_slab = pltpu.make_async_copy(h_ref, slabs.at[row], own_sem.at[1])
    own_panel.start()
    own_slab.start()
    clear_corner(right_parts, h_ref.shape[0])
    own_lists.wait()
    own_live.wait()
    table[...] = jnp.zeros(table.shape, jnp.int32)
    for index in range(STEPS):
        sort_pairs(lists, live[0, index], index, table)
    moved = pltpu.make_async_copy(table, slots, own_sem.at[3])
    moved.start()
    moved.wait()
    own_panel.wait()
    own_slab.wait()

    def products(index, first, low, rows):
        part = pl.ds(low, rows)

        def body(block, acc):
            start = block * GROUP
            found = []
            for k in range(GROUP):
                found.append(
                    multiply(
                        left_parts[slots[8 * index, start + k], part, :],
                        right_parts[slots[8 * index + 1, start + k]],
                    )
                )
            for k in range(GROUP):
                acc = acc * slots[8 * index + 2, start + k].astype(jnp.float32) + found[k]
                runs[start + k, part, :] = acc
            return acc

        lax.fori_loop(0, width // GROUP, body, jnp.zeros((rows, 128), jnp.float32))

        def collect(j, carry):
            term = runs[slots[8 * index + 3, j], part, :] * slots[8 * index + 4, j].astype(jnp.float32)
            c_ref[j, part, :] = term if first else c_ref[j, part, :] + term
            return carry

        lax.fori_loop(0, c_ref.shape[0], collect, 0)

    def out_copy(low, rows, which):
        part = pl.ds(low, rows)
        return pltpu.make_async_copy(c_ref.at[:, part], out_ref.at[:, part], out_sem.at[which])

    def take(distance, q):
        @pl.when(col + distance <= 3)
        def _():
            panel_copy(col + distance, q, True).wait_recv()

            @pl.when(col > 0)
            def _():
                panel_copy(col + distance, q, True).start()

        @pl.when(col - distance >= 0)
        def _():
            panel_copy(col - distance, q, False).wait_recv()

            @pl.when(col < 3)
            def _():
                panel_copy(col - distance, q, False).start()

    split_left(panels.at[col], left_parts, 0, 128)
    split_right(slabs.at[row], right_parts, 0, h_ref.shape[0])
    products(0, True, 0, 128)
    for distance in (1, 2):
        for q in range(CHUNKS):
            take(distance, q)
    slab_copy(sibling, 1, sibling).wait_recv()
    slab_copy(across, 0, across).wait_recv()
    slab_copy(across, 2, sibling).start()
    slab_copy(diagonal, 2, sibling).wait_recv()
    for i in range(1, STEPS):
        index = jnp.where(col < 2, i, STEPS - i)
        split_right(slabs.at[(row + index) % 4], right_parts, 0, h_ref.shape[0])
        left = panels.at[(col + index) % 4]
        if i < STEPS - 1:
            split_left(left, left_parts, 0, 128)
            products(index, False, 0, 128)
            continue
        for q in range(CHUNKS - 1):
            take(3, q)
        early = 128 - piece
        split_left(left, left_parts, 0, early)
        products(index, False, 0, early)
        out_copy(0, early, 0).start()
        take(3, CHUNKS - 1)
        split_left(left, left_parts, early, piece)
        products(index, False, early, piece)
        out_copy(early, piece, 1).start()
        out_copy(0, early, 0).wait()
        out_copy(early, piece, 1).wait()

    for tile in range(4):
        for q in range(CHUNKS):
            @pl.when(jnp.logical_and(col > 0, tile >= col))
            def _():
                panel_copy(tile, q, True).wait_send()

            @pl.when(jnp.logical_and(col < 3, tile <= col))
            def _():
                panel_copy(tile, q, False).wait_send()

    slab_copy(row, 0, across).wait_send()
    slab_copy(row, 1, sibling).wait_send()
    slab_copy(across, 2, sibling).wait_send()


def ring(p_tiles, h_tiles, pair_lists, pair_counts):
    count, slabs = p_tiles.shape[0], h_tiles.shape[0]
    dma = pltpu.SemaphoreType.DMA
    return pl.pallas_call(
        ring_kernel,
        out_shape=jax.ShapeDtypeStruct((CAPC, 128, 128), jnp.float32),
        in_specs=[pl.BlockSpec(memory_space=pltpu.HBM)] * 4,
        out_specs=pl.BlockSpec(memory_space=pl.ANY),
        scratch_shapes=[
            pltpu.SMEM((1, STEPS), jnp.int32),
            pltpu.VMEM(pair_lists.shape, jnp.int32),
            pltpu.VMEM((8 * STEPS, 128), jnp.int32),
            pltpu.SMEM((8 * STEPS, 128), jnp.int32),
            pltpu.VMEM((CAPC, 128, 128), jnp.float32),
            pltpu.VMEM((4, count, 128, 128), jnp.float32),
            pltpu.VMEM((4, slabs, 128, 128), jnp.float32),
            pltpu.VMEM((count, 128, 256), jnp.bfloat16),
            pltpu.VMEM((slabs, 256, 256), jnp.bfloat16),
            pltpu.VMEM((pair_lists.shape[1], 128, 128), jnp.float32),
            dma((5,)),
            dma((2,)),
            dma((4, CHUNKS)),
            dma((4, CHUNKS)),
            dma((4, CHUNKS)),
            dma((3,)),
            dma((4,)),
        ],
        compiler_params=pltpu.CompilerParams(
            collective_id=0, has_side_effects=True, vmem_limit_bytes=60 << 20
        ),
        cost_estimate=pl.CostEstimate(
            flops=STEPS * 96 * 2 * 128 * 256 * 256, bytes_accessed=12 << 20, transcendentals=0
        ),
    )(pair_counts.T, pair_lists, p_tiles, h_tiles)


def shards(p_tiles, h_tiles, pair_lists, pair_counts):
    if lax.axis_size("row") == 4 and lax.axis_size("col") == 4:
        return ring(p_tiles, h_tiles, pair_lists, pair_counts)
    accum = jnp.zeros((CAPC, p_tiles.shape[1], p_tiles.shape[2]), jnp.float32)
    panel_tile = p_tiles
    slab_tile = h_tiles
    for index in range(STEPS):
        if index > 0:
            panel_tile = from_behind(panel_tile, "col", -1)
            slab_tile = from_behind(slab_tile, "row", -1)
        lists = pair_lists[3 * index : 3 * index + 3]
        accum = step(panel_tile, slab_tile, lists, pair_counts[index], accum)
    return accum


def solution(mesh):
    placed = (
        P(("groups", "row"), "col", None),
        P(("groups", "row"), "col", None),
        P(("groups", "row"), "col"),
        P(("groups", "row"), "col"),
    )
    return jax.shard_map(
        shards,
        mesh=mesh,
        in_specs=placed,
        out_specs=P(("groups", "row"), "col", None),
        check_vma=False,
    )
```

```python
import functools

import jax
import jax.numpy as jnp
from jax import lax
from jax.experimental import pallas as pl
from jax.experimental.pallas import tpu as pltpu
from jax.sharding import PartitionSpec as P

STEPS = 4
CAPC = 48
GROUP = 8


def from_behind(value, axis, steps):
    count = lax.axis_size(axis)
    pairs = [(source, (source + steps) % count) for source in range(count)]
    return lax.ppermute(value, axis, pairs)


def split(value):
    high = value.astype(jnp.bfloat16)
    low = (value - high.astype(jnp.float32)).astype(jnp.bfloat16)
    return high, low


def split_left(source, target, first, rows):
    part = pl.ds(first, rows)

    def body(slot, carry):
        high, low = split(source[slot, part, :])
        target[slot, part, 0:128] = high
        target[slot, part, 128:256] = low
        return carry

    lax.fori_loop(0, source.shape[0], body, 0)


def split_right(source, target, first, count):
    def body(slot, carry):
        high, low = split(source[slot])
        target[slot, 0:128, 0:128] = high
        target[slot, 0:128, 128:256] = low
        target[slot, 128:256, 0:128] = high
        return carry

    lax.fori_loop(first, first + count, body, 0)


def clear_corner(target, count):
    def body(slot, carry):
        target[slot, 128:256, 128:256] = jnp.zeros((128, 128), jnp.bfloat16)
        return carry

    lax.fori_loop(0, count, body, 0)


def multiply(left, right):
    both = jnp.dot(left, right, preferred_element_type=jnp.float32)
    return both[:, 0:128] + both[:, 128:256]


def step_kernel(lists, live, left, right, before, after, left_parts, right_parts):
    split_left(left, left_parts, 0, left.shape[1])
    clear_corner(right_parts, right.shape[0])
    split_right(right, right_parts, 0, right.shape[0])
    after[...] = before[...]
    count = live[0]

    def body(group, carry):
        first = group * GROUP
        products = []
        for k in range(GROUP):
            product = multiply(left_parts[lists[0, first + k]], right_parts[lists[1, first + k]])
            products.append(jnp.where(first + k < count, product, 0.0))
        for k in range(GROUP):
            place = lists[2, first + k]
            after[place] = after[place] + products[k]
        return carry

    lax.fori_loop(0, (count + GROUP - 1) // GROUP, body, 0)


def step(left, right, lists, live, before):
    width = lists.shape[1]
    return pl.pallas_call(
        step_kernel,
        out_shape=jax.ShapeDtypeStruct(before.shape, jnp.float32),
        in_specs=[
            pl.BlockSpec(memory_space=pltpu.SMEM),
            pl.BlockSpec(memory_space=pltpu.SMEM),
            pl.BlockSpec(memory_space=pltpu.VMEM),
            pl.BlockSpec(memory_space=pltpu.VMEM),
            pl.BlockSpec(memory_space=pltpu.VMEM),
        ],
        out_specs=pl.BlockSpec(memory_space=pltpu.VMEM),
        scratch_shapes=[
            pltpu.VMEM((left.shape[0], 128, 256), jnp.bfloat16),
            pltpu.VMEM((right.shape[0], 256, 256), jnp.bfloat16),
        ],
        compiler_params=pltpu.CompilerParams(vmem_limit_bytes=40 << 20),
        cost_estimate=pl.CostEstimate(
            flops=width * 2 * 128 * 256 * 256, bytes_accessed=12 << 20, transcendentals=0
        ),
    )(lists, live, left, right, before)


CHUNKS = 4
MESH = pl.DeviceIdType.MESH


def sort_pairs(lists, count, index, table):
    width = lists.shape[1]
    lane = lax.broadcasted_iota(jnp.int32, (width, width), 1)
    diagonal = lax.broadcasted_iota(jnp.int32, (width, width), 0) == lane
    slot = lax.broadcasted_iota(jnp.int32, (1, width), 1)

    def column(line):
        return jnp.sum(jnp.where(diagonal, line, 0), axis=1, keepdims=True)

    def total(mask, values):
        return jnp.sum(jnp.where(mask, values, 0), axis=0, keepdims=True)

    triple = [lists[3 * index + role : 3 * index + role + 1, :] for role in range(3)]
    place = jnp.where(slot < count, triple[2], CAPC)
    order = place * width + slot
    rank = jnp.sum((order < column(order)).astype(jnp.int32), axis=1, keepdims=True)
    place_column = column(place)
    hit = rank == lane
    target = total(hit, place_column)
    behind = jnp.where(slot == 0, -1, total(rank == lane - 1, place_column))
    lines = (
        total(hit, column(triple[0])),
        total(hit, column(triple[1])),
        (target == behind).astype(jnp.int32),
        jnp.maximum(total(place_column <= lane, 1) - 1, 0),
        jnp.minimum(total(place_column == lane, 1), 1),
    )
    for role, line in enumerate(lines):
        table[8 * index + role : 8 * index + role + 1, 0:width] = line


def ring_kernel(
    live_ref, lists_ref, p_ref, h_ref, out_ref,
    live, lists, table, slots, c_ref, panels, slabs, left_parts, right_parts, runs,
    own_sem, out_sem, p_left, p_right, p_recv, h_send, h_recv,
):
    group = lax.axis_index("groups")
    row = lax.axis_index("row")
    col = lax.axis_index("col")
    piece = p_ref.shape[1] // CHUNKS
    width = lists_ref.shape[1]
    sibling = row + 1 - 2 * (row % 2)
    across = (row + 2) % 4
    diagonal = (sibling + 2) % 4

    barrier = pltpu.get_barrier_semaphore()

    def greet(r, c):
        pl.semaphore_signal(barrier, inc=1, device_id=(group, r, c), device_id_type=MESH)

    greet(sibling, col)
    greet(across, col)

    @pl.when(col > 0)
    def _():
        greet(row, col - 1)

    @pl.when(col < 3)
    def _():
        greet(row, col + 1)

    pl.semaphore_wait(barrier, 2 + jnp.minimum(col, 1) + jnp.minimum(3 - col, 1))

    def panel_copy(tile, q, leftward, own=False):
        part = pl.ds(q * piece, piece)
        return pltpu.make_async_remote_copy(
            src_ref=p_ref.at[:, part] if own else panels.at[tile, :, part],
            dst_ref=panels.at[tile, :, part],
            send_sem=p_left.at[tile, q] if leftward else p_right.at[tile, q],
            recv_sem=p_recv.at[tile, q],
            device_id=(group, row, (col + 3) % 4 if leftward else (col + 1) % 4),
            device_id_type=MESH,
        )

    def slab_copy(tile, which, target, own=False):
        return pltpu.make_async_remote_copy(
            src_ref=h_ref if own else slabs.at[tile],
            dst_ref=slabs.at[tile],
            send_sem=h_send.at[which],
            recv_sem=h_recv.at[tile],
            device_id=(group, target, col),
            device_id_type=MESH,
        )

    for q in range(CHUNKS):
        @pl.when(col > 0)
        def _():
            panel_copy(col, q, True, True).start()

        @pl.when(col < 3)
        def _():
            panel_copy(col, q, False, True).start()

    slab_copy(row, 0, across, True).start()
    slab_copy(row, 1, sibling, True).start()
    own_lists = pltpu.make_async_copy(lists_ref, lists, own_sem.at[2])
    own_lists.start()
    own_live = pltpu.make_async_copy(live_ref, live, own_sem.at[4])
    own_live.start()
    own_panel = pltpu.make_async_copy(p_ref, panels.at[col], own_sem.at[0])
    own_slab = pltpu.make_async_copy(h_ref, slabs.at[row], own_sem.at[1])
    own_panel.start()
    own_slab.start()
    clear_corner(right_parts, h_ref.shape[0])
    own_lists.wait()
    own_live.wait()
    table[...] = jnp.zeros(table.shape, jnp.int32)
    for index in range(STEPS):
        sort_pairs(lists, live[0, index], index, table)
    moved = pltpu.make_async_copy(table, slots, own_sem.at[3])
    moved.start()
    moved.wait()
    own_panel.wait()
    own_slab.wait()

    def products(index, first, low, rows):
        part = pl.ds(low, rows)

        def body(block, acc):
            start = block * GROUP
            found = []
            for k in range(GROUP):
                found.append(
                    multiply(
                        left_parts[slots[8 * index, start + k], part, :],
                        right_parts[slots[8 * index + 1, start + k]],
                    )
                )
            for k in range(GROUP):
                acc = acc * slots[8 * index + 2, start + k].astype(jnp.float32) + found[k]
                runs[start + k, part, :] = acc
            return acc

        lax.fori_loop(0, width // GROUP, body, jnp.zeros((rows, 128), jnp.float32))

        def collect(j, carry):
            term = runs[slots[8 * index + 3, j], part, :] * slots[8 * index + 4, j].astype(jnp.float32)
            c_ref[j, part, :] = term if first else c_ref[j, part, :] + term
            return carry

        lax.fori_loop(0, c_ref.shape[0], collect, 0)

    def out_copy(low, rows, which):
        part = pl.ds(low, rows)
        return pltpu.make_async_copy(c_ref.at[:, part], out_ref.at[:, part], out_sem.at[which])

    def take(distance, q):
        @pl.when(col + distance <= 3)
        def _():
            panel_copy(col + distance, q, True).wait_recv()

            @pl.when(col > 0)
            def _():
                panel_copy(col + distance, q, True).start()

        @pl.when(col - distance >= 0)
        def _():
            panel_copy(col - distance, q, False).wait_recv()

            @pl.when(col < 3)
            def _():
                panel_copy(col - distance, q, False).start()

    split_left(panels.at[col], left_parts, 0, 128)
    split_right(slabs.at[row], right_parts, 0, h_ref.shape[0])
    products(0, True, 0, 128)
    for distance in (1, 2):
        for q in range(CHUNKS):
            take(distance, q)
    slab_copy(sibling, 1, sibling).wait_recv()
    slab_copy(across, 0, across).wait_recv()
    slab_copy(across, 2, sibling).start()
    slab_copy(diagonal, 2, sibling).wait_recv()
    for i in range(1, STEPS):
        index = jnp.where(col < 2, i, STEPS - i)
        split_right(slabs.at[(row + index) % 4], right_parts, 0, h_ref.shape[0])
        left = panels.at[(col + index) % 4]
        if i < STEPS - 1:
            split_left(left, left_parts, 0, 128)
            products(index, False, 0, 128)
            continue
        for q in range(CHUNKS - 1):
            take(3, q)
        early = 128 - piece
        split_left(left, left_parts, 0, early)
        products(index, False, 0, early)
        out_copy(0, early, 0).start()
        take(3, CHUNKS - 1)
        split_left(left, left_parts, early, piece)
        products(index, False, early, piece)
        out_copy(early, piece, 1).start()
        out_copy(0, early, 0).wait()
        out_copy(early, piece, 1).wait()

    for tile in range(4):
        for q in range(CHUNKS):
            @pl.when(jnp.logical_and(col > 0, tile >= col))
            def _():
                panel_copy(tile, q, True).wait_send()

            @pl.when(jnp.logical_and(col < 3, tile <= col))
            def _():
                panel_copy(tile, q, False).wait_send()

    slab_copy(row, 0, across).wait_send()
    slab_copy(row, 1, sibling).wait_send()
    slab_copy(across, 2, sibling).wait_send()


def ring(p_tiles, h_tiles, pair_lists, pair_counts):
    count, slabs = p_tiles.shape[0], h_tiles.shape[0]
    dma = pltpu.SemaphoreType.DMA
    return pl.pallas_call(
        ring_kernel,
        out_shape=jax.ShapeDtypeStruct((CAPC, 128, 128), jnp.float32),
        in_specs=[pl.BlockSpec(memory_space=pltpu.HBM)] * 4,
        out_specs=pl.BlockSpec(memory_space=pl.ANY),
        scratch_shapes=[
            pltpu.SMEM((1, STEPS), jnp.int32),
            pltpu.VMEM(pair_lists.shape, jnp.int32),
            pltpu.VMEM((8 * STEPS, 128), jnp.int32),
            pltpu.SMEM((8 * STEPS, 128), jnp.int32),
            pltpu.VMEM((CAPC, 128, 128), jnp.float32),
            pltpu.VMEM((4, count, 128, 128), jnp.float32),
            pltpu.VMEM((4, slabs, 128, 128), jnp.float32),
            pltpu.VMEM((count, 128, 256), jnp.bfloat16),
            pltpu.VMEM((slabs, 256, 256), jnp.bfloat16),
            pltpu.VMEM((pair_lists.shape[1], 128, 128), jnp.float32),
            dma((5,)),
            dma((2,)),
            dma((4, CHUNKS)),
            dma((4, CHUNKS)),
            dma((4, CHUNKS)),
            dma((3,)),
            dma((4,)),
        ],
        compiler_params=pltpu.CompilerParams(
            collective_id=0, has_side_effects=True, vmem_limit_bytes=60 << 20
        ),
        cost_estimate=pl.CostEstimate(
            flops=STEPS * 96 * 2 * 128 * 256 * 256, bytes_accessed=12 << 20, transcendentals=0
        ),
    )(pair_counts.T, pair_lists, p_tiles, h_tiles)


def shards(p_tiles, h_tiles, pair_lists, pair_counts):
    if lax.axis_size("row") == 4 and lax.axis_size("col") == 4:
        return ring(p_tiles, h_tiles, pair_lists, pair_counts)
    accum = jnp.zeros((CAPC, p_tiles.shape[1], p_tiles.shape[2]), jnp.float32)
    panel_tile = p_tiles
    slab_tile = h_tiles
    for index in range(STEPS):
        if index > 0:
            panel_tile = from_behind(panel_tile, "col", -1)
            slab_tile = from_behind(slab_tile, "row", -1)
        lists = pair_lists[3 * index : 3 * index + 3]
        accum = step(panel_tile, slab_tile, lists, pair_counts[index], accum)
    return accum


def solution(mesh):
    placed = (
        P(("groups", "row"), "col", None),
        P(("groups", "row"), "col", None),
        P(("groups", "row"), "col"),
        P(("groups", "row"), "col"),
    )
    return jax.shard_map(
        shards,
        mesh=mesh,
        in_specs=placed,
        out_specs=P(("groups", "row"), "col", None),
        check_vma=False,
    )
```
